1024 devices in a mesh: replica: 16 (over z_lo), expert: 64 (over z_hi, y, x, core).
Axes of the slice: x: 4, y: 4, z: 32 (z_hi: 2, z_lo: 16; z = z_hi * 16 + z_lo), core: 2. Of those that a mesh axis runs over, the one named last changes fastest.
Arguments:
- tokens: bfloat16 [16, 8192, 2560], P('replica', 'expert'), may hold values from -6 to 6
- routes: int32 [16, 8192, 2], P('replica', 'expert'), may hold values from 0 to 63, all different within a row; in each aligned block of 128 rows (0 to 127, 128 to 255, ..., all dimensions but the last counted through in order) at most 6 rows name the same one
- route_weight: float32 [16, 8192, 2], P('replica', 'expert'), may hold values from 0.2 to 1
- gate_weight: bfloat16 [64, 2560, 768], P('expert'), may hold values from -0.125 to 0.125
- up_weight: bfloat16 [64, 2560, 768], P('expert'), may hold values from -0.125 to 0.125
- local_params: bfloat16 [16, 2048, 2048], P('replica', 'expert'), may hold values from -6 to 6
- base: float32 [2048, 2048], P('expert'), may hold values from -6 to 6
- momentum: float32 [2048, 2048], P('expert'), may hold values from -3 to 3
Outputs:
- mixed: bfloat16 [16, 8192, 2, 768], P('replica', 'expert')
- new_base: float32 [2048, 2048], P('expert')
- new_momentum: float32 [2048, 2048], P('expert')
The draws below stay inside these ranges and needn't reach their ends.
Inputs may be any that keep to these rules, and one draw needn't show every extreme that they name: `routes`: the 2 experts of a token differ; the rows of one device name each expert at most 6 times, and some device names some expert exactly 6 times.
All inputs are finite; a program needn't handle non-finite values.
Results may differ from the reference program's by a relative error of at most 0.0049.
Values may be sent and summed in bfloat16 or wider, within the bound.
A program may use at most 32 MiB of HBM per device.

```python
import math
import jax
import jax.numpy as jnp
import numpy as np
from jax import lax

DW = 2560
HW = 768
TOPK = 2
TOK_DEV = 128
FC = 2048
EXPERTS = 64
CAP = 6
TOKENS = 8192
FRAG_R = 2048
N_REPLICA = 16
N_EXPERT = 64


def shard_levels(own_key, dims, shards, least, high):
    gain, own = 1.0, jax.random.fold_in(own_key, 6)
    for position, shards_of in shards:
        steps = jnp.exp(jax.random.uniform(jax.random.fold_in(own, position), (shards_of,), jnp.float32, least / len(shards), high / len(shards)))
        gain = gain * jnp.repeat(steps, dims[position] // shards_of).reshape([-1 if axis == position else 1 for axis in range(len(dims))])
    return gain


def deal_out(key, own, number, rows, amount, top, most, slope):
    order = jax.random.permutation(key, amount)
    packed, ordinary = shares(amount, rows * top, most, slope, True), shares(amount, rows * top, most, slope, False)
    places = jnp.arange(amount)

    def named(lengths, offset_by):
        used = int((lengths > 0).sum())
        fixed = max(1, used // 4)
        moved = fixed + (places - fixed + offset_by * (used - fixed)) % max(1, amount - fixed)
        return jnp.zeros((amount,), jnp.int32).at[order[jnp.where(places < fixed, places, moved)]].set(jnp.asarray(lengths, jnp.int32))

    lengths = jnp.where(number % 4 == 0, named(packed, number // 4), named(ordinary, number - number // 4 - 1))
    mixed = jax.random.permutation(jax.random.fold_in(own, 3), amount)
    source_of, taker = mixed[0:amount // 2 * 2:2], mixed[1:amount // 2 * 2:2]
    slack = jnp.minimum(lengths[source_of] - 1, most - lengths[taker]) // 2
    slack = jnp.where((source_of == order[0]) | (taker == order[0]) | (lengths[taker] == 0), 0, jnp.maximum(slack, 0))
    moved = jax.random.randint(jax.random.fold_in(own, 4), (amount // 2,), 0, 1 << 20) % (slack + 1)
    lengths = lengths.at[source_of].add(-moved).at[taker].add(moved)
    members = jnp.searchsorted(jnp.cumsum(lengths), jnp.arange(rows * top), side="right").astype(jnp.int32)
    table = members.reshape(top, rows).T
    table = table[jax.random.permutation(jax.random.fold_in(own, 1), rows)]
    offset_by = jax.random.randint(jax.random.fold_in(own, 2), (rows, 1), 0, top)
    return jnp.take_along_axis(table, (jnp.arange(top)[None, :] + offset_by) % top, axis=1)


def shares(amount, total, bound, slope, full):
    weights = [(1 << 20) // math.isqrt(grade ** slope) + 1 for grade in range(1, amount + 1)]
    largest = bound if full else min(bound, max(-(-total // amount), total * weights[0] // sum(weights)))
    least = 1 if total - largest >= amount - 1 else 0
    counts, surplus = [largest] + [least] * (amount - 1), total - largest - least * (amount - 1)
    while surplus > 0:
        free = [i for i in range(1, amount) if counts[i] < largest] or [i for i in range(1, amount) if counts[i] < bound]
        whole, remaining = sum([weights[i] for i in free]), surplus
        for i in free:
            more = min(bound - counts[i], max(1, remaining * weights[i] // whole), surplus)
            counts[i] = counts[i] + more
            surplus = surplus - more
    return np.array(counts)


def gaussian(key, shape, scale, most, pieces=(), kind=jnp.bfloat16):
    loudness = shard_levels(key, shape, pieces, -0.22, 0.18) if pieces else 1.0
    entries = jax.random.normal(key, shape, jnp.float32) * scale * loudness
    return jnp.minimum(jnp.maximum(entries, -most), most).astype(kind)


def setup_inputs(seed: int = 0) -> dict:
    key_list = jax.random.split(jax.random.key(seed), 9)
    tokens = gaussian(key_list[0], (N_REPLICA, TOKENS, DW), 1.0, 6.0, ((0, 16), (1, 64)))
    routes_keys = jax.random.split(jax.random.fold_in(key_list[1], 1), N_REPLICA * TOKENS // TOK_DEV)
    routes_turns = jax.random.permutation(jax.random.fold_in(key_list[1], 3), N_REPLICA * TOKENS // TOK_DEV)
    routes = jax.vmap(lambda own, number: deal_out(jax.random.fold_in(key_list[1], 2), own, number, TOK_DEV, EXPERTS, TOPK, CAP, 1))(routes_keys, routes_turns).reshape((N_REPLICA, TOKENS, TOPK))
    route_weight = jnp.clip(jnp.exp(math.log(1.0) - 1.609438 * jax.random.uniform(key_list[2], (N_REPLICA, TOKENS, TOPK), jnp.float32) ** shard_levels(key_list[2], (N_REPLICA, TOKENS, TOPK), ((0, 16), (1, 64)), -0.2, 0.2)), 0.2, 1.0)
    gate_weight = gaussian(key_list[3], (EXPERTS, DW, HW), DW ** -0.5, 0.125, ((0, 64),))
    up_weight = gaussian(key_list[4], (EXPERTS, DW, HW), DW ** -0.5, 0.125, ((0, 64),))
    local_params = gaussian(key_list[5], (N_REPLICA, FRAG_R, FC), 1.0, 6.0, ((0, 16), (1, 64)))
    base = gaussian(key_list[6], (FRAG_R, FC), 1.0, 6.0, ((0, 64),), jnp.float32)
    momentum = gaussian(key_list[7], (FRAG_R, FC), 0.5, 3.0, ((0, 64),), jnp.float32)
    return {"tokens": tokens, "routes": routes, "route_weight": route_weight, "gate_weight": gate_weight, "up_weight": up_weight, "local_params": local_params, "base": base, "momentum": momentum}


outer_rate = 0.7
outer_beta = 0.9


def expert_rows(args):
    block, w_gate, w_up = args
    gate = jnp.dot(block, w_gate, preferred_element_type=jnp.float32)
    upper = jnp.dot(block, w_up, preferred_element_type=jnp.float32)
    return (jax.nn.silu(gate) * upper).astype(jnp.bfloat16)


def one_replica(gate_weight, up_weight):
    def inner(args):
        rows, chosen, weights = args
        pairs = chosen.reshape(N_EXPERT, TOK_DEV * TOPK)
        onehot = (pairs[:, :, None] == jnp.arange(EXPERTS, dtype=jnp.int32)[None, None, :]).astype(jnp.int32)
        ranks = jnp.sum((jnp.cumsum(onehot, axis=1) - onehot) * onehot, axis=2).astype(jnp.int32)
        source = jnp.arange(N_EXPERT, dtype=jnp.int32)[:, None]
        index = (pairs * (N_EXPERT * CAP) + source * CAP + ranks).reshape(-1).astype(jnp.int32)
        token_of = (jnp.arange(TOKENS * TOPK, dtype=jnp.int32) // TOPK).astype(jnp.int32)
        buffer = jnp.zeros((EXPERTS * N_EXPERT * CAP, DW), jnp.bfloat16).at[index].set(rows[token_of])
        buffer = buffer.reshape(EXPERTS, N_EXPERT * CAP, DW)
        hidden = lax.map(expert_rows, (buffer, gate_weight, up_weight))
        picked = hidden.reshape(EXPERTS * N_EXPERT * CAP, HW)[index]
        mixed = (weights.reshape(-1, 1) * picked.astype(jnp.float32)).astype(jnp.bfloat16)
        return mixed.reshape(TOKENS, TOPK, HW)
    return inner


def reference(tokens, routes, route_weight, gate_weight, up_weight, local_params, base, momentum):
    mixed = lax.map(one_replica(gate_weight, up_weight), (tokens, routes, route_weight))
    delta = (base[None, :, :] - local_params.astype(jnp.float32)).astype(jnp.bfloat16)
    delta = lax.optimization_barrier(delta)
    outer_grad = jnp.sum(delta.astype(jnp.float32), axis=0) / N_REPLICA
    new_momentum = outer_beta * momentum + outer_grad
    new_base = base - outer_rate * (outer_grad + outer_beta * new_momentum)
    return mixed, new_base, new_momentum
```

```python
import jax
import jax.numpy as jnp
from jax import lax
from jax.experimental import pallas as pl
from jax.experimental.pallas import tpu as pltpu
from jax.sharding import PartitionSpec as P

MESH = pl.DeviceIdType.MESH
outer_rate = 0.7
outer_beta = 0.9

LINE = 16
PLANE = 32
ROWS = 16
TOK, DW, HW = 128, 2560, 768
CB = 256
NJ = HW // CB
CHUNK = 128
NR = DW // CHUNK
NB = 2 * NR
M = NJ * NB
SHIFT = 8
LEAD = 6
LAG = 45
PIECES = 4
CEN = 8
HOP = 3


def received(a):
    return M // 2 + ((LINE - 1 - 2 * a) * SHIFT) // 8


def kernel(tok, routes, weights, gate_hbm, up_hbm, local, base, mixed, total,
           own, oth, rel, outg, recvd, own_hid, hid, ret, pick, part, acc, xin,
           load_sem, recv_d, recv_r, fwd_d, fwd_r, x_s, own_r,
           disp_s, disp_r, ret_s, ret_r, loc_s, in_r, in_s, xin_r, xin_s, tot_r, tot_s):
    i = lax.axis_index("replica")
    e = lax.axis_index("expert")
    d = lax.rem(e, 2)
    half = e // PLANE
    me = lax.rem(e, PLANE)
    flip = lax.rem(e + PLANE, 2 * PLANE)
    mate = e + 1 - 2 * d
    mflip = lax.rem(mate + PLANE, 2 * PLANE)
    last = LINE - 1
    k = jnp.where(d == 0, i, last - i)
    end = jnp.where(d == 0, last, 0)
    way = 1 - 2 * d
    ni = lax.rem(i + way + LINE, LINE)
    pi = lax.rem(i - way + LINE, LINE)
    nxt = (ni, jnp.where(i == end, flip, e))
    prv = (pi, jnp.where(i == last - end, flip, e))
    opp = (pi, mflip)
    mid = (i, mate)

    def count(a):
        return jnp.where(d == 0, received(a), M - received(last - a))

    wopp = jnp.where(d == 0, M - received(last), received(0))

    def peer(n):
        q = lax.rem(me + 1 + n, PLANE)
        return q, (i, half * PLANE + q)

    barrier = pltpu.get_barrier_semaphore()
    for dev in (nxt, prv):
        pl.semaphore_signal(barrier, inc=1, device_id=dev, device_id_type=MESH)

    @pl.when(k == 0)
    def _():
        pl.semaphore_signal(barrier, inc=1, device_id=opp, device_id_type=MESH)

    loads = []
    for j in (0, *range(NJ - 1, 0, -1)):
        for g, ref in enumerate((gate_hbm, up_hbm)):
            loads.append(pltpu.make_async_copy(ref.at[:, pl.ds(j * CB, CB)], own.at[j, g], load_sem.at[j, g]))
    for copy in loads:
        copy.start()

    def greet(n, _):
        pl.semaphore_signal(barrier, inc=1, device_id=peer(n)[1], device_id_type=MESH)
        return 0

    lax.fori_loop(0, PLANE - 1, greet, 0)
    pl.semaphore_wait(barrier, PLANE + 1 + jnp.where(k == 0, 1, 0))
    for copy in loads:
        copy.wait()

    def at(buf, c):
        rows = pl.ds(pl.multiple_of(lax.rem(c, NB) // 2 * CHUNK, CHUNK), CHUNK)
        return buf.at[c // NB, lax.rem(c, 2), rows, :]

    def cp(src, dst, c, ss, rs, dev):
        return pltpu.make_async_remote_copy(src_ref=at(src, c), dst_ref=at(dst, c), send_sem=ss.at[c],
                                            recv_sem=rs.at[c], device_id=dev, device_id_type=MESH)

    def mine(s):
        return jnp.where(d == 0, s, M - 1 - s)

    def theirs(s):
        return jnp.where(d == 0, M - 1 - s, s)

    def opp_send(s):
        return cp(own, rel, theirs(s), own_r, recv_r, opp)

    def first_send(s):
        return cp(own, oth, mine(s), fwd_d, recv_d, nxt)

    def lead_body(s, _):
        pl.when(k == 0)(lambda: opp_send(s).start())
        pl.when(k == last)(lambda: first_send(s).start())
        return 0

    lax.fori_loop(0, LEAD, lead_body, 0)

    lanes = lax.broadcasted_iota(jnp.int32, (TOK, 2 * PLANE), 1)
    r = [routes[:, 0:1], routes[:, 1:2]]
    named = ((r[0] == lanes) | (r[1] == lanes)).astype(jnp.float32)
    before = (lax.broadcasted_iota(jnp.int32, (TOK, TOK), 1) < lax.broadcasted_iota(jnp.int32, (TOK, TOK), 0))
    ranks = jnp.dot(before.astype(jnp.bfloat16), named.astype(jnp.bfloat16), preferred_element_type=jnp.float32)
    slots = lax.broadcasted_iota(jnp.int32, (TOK, PLANE * ROWS), 1)
    place = jnp.zeros((TOK, PLANE * ROWS), jnp.float32)
    for t in range(2):
        rank = jnp.sum(jnp.where(r[t] == lanes, ranks, 0.0), axis=1, keepdims=True).astype(jnp.int32)
        row = (r[t] & (PLANE - 1)) * ROWS + jnp.where(r[t] // PLANE == half, 0, ROWS // 2) + rank
        one = (row == slots).astype(jnp.float32)
        pick[t] = one.astype(jnp.bfloat16)
        place += one
    place_t = place.T.astype(jnp.bfloat16)
    for c in range(DW // 512):
        cols = pl.ds(c * 512, 512)
        outg[:, cols] = jnp.dot(place_t, tok[:, cols], preferred_element_type=jnp.float32).astype(jnp.bfloat16)

    def block(q):
        return pl.ds(pl.multiple_of(q * ROWS, ROWS), ROWS)

    def dispatch(n):
        q, dev = peer(n)
        pltpu.make_async_remote_copy(src_ref=outg.at[block(q)], dst_ref=recvd.at[block(me)], send_sem=disp_s,
                                     recv_sem=disp_r, device_id=dev, device_id_type=MESH).start()

    own_rows = pltpu.make_async_copy(outg.at[block(me)], recvd.at[block(me)], loc_s.at[0])
    own_rows.start()

    @pl.when(k >= 8)
    def _():
        def body(n, _):
            dispatch(n)
            return 0
        lax.fori_loop(0, PLANE - 1, body, 0)

    width = part.shape[2]

    def pcopy(src, dst, c, ss, rs, dev):
        return pltpu.make_async_remote_copy(src_ref=src.at[c], dst_ref=dst.at[c], send_sem=ss.at[c],
                                            recv_sem=rs.at[c], device_id=dev, device_id_type=MESH)

    for c in range(PIECES):
        cols = pl.ds(c * width, width)
        delta = (base[:, cols] - local[:, cols].astype(jnp.float32)).astype(jnp.bfloat16)
        acc[c] = delta.astype(jnp.float32)

    @pl.when(k > CEN)
    def _():
        for c in range(PIECES):
            @pl.when(k < last)
            def _():
                pcopy(acc, part, c, in_s, in_r, prv).wait_recv()
                acc[c] = acc[c] + part[c]

            pl.when(k > CEN + 1)(lambda: pcopy(acc, part, c, in_s, in_r, prv).start())
            pl.when(k == CEN + 1)(lambda: pcopy(acc, xin, c, xin_s, xin_r, prv).start())

    def deltas(s):
        low = k <= CEN

        @pl.when(low & (s < PIECES))
        def _():
            @pl.when(k > 0)
            def _():
                pcopy(acc, part, s, in_s, in_r, nxt).wait_recv()
                acc[s] = acc[s] + part[s]

            pl.when(k < CEN)(lambda: pcopy(acc, part, s, in_s, in_r, nxt).start())
            pl.when(k == CEN)(lambda: pcopy(acc, xin, s, xin_s, xin_r, nxt).start())

        meet = s - jnp.where(low, 6, 1)

        @pl.when(((k == CEN) | (k == CEN + 1)) & (meet >= 0) & (meet < PIECES))
        def _():
            pcopy(acc, xin, meet, xin_s, xin_r, nxt).wait_recv()
            total[meet] = acc[meet] + xin[meet]
            pl.when(low)(lambda: pcopy(total, total, meet, tot_s, tot_r, prv).start())
            pl.when(k > CEN)(lambda: pcopy(total, total, meet, tot_s, tot_r, nxt).start())

        back = s - jnp.where(low, 2 * HOP * (CEN - k) + 6, 2)

        @pl.when(((k < CEN) | (k > CEN + 1)) & (back >= 0) & (back < PIECES))
        def _():
            pcopy(total, total, back, tot_s, tot_r, prv).wait_recv()
            pl.when((k < CEN) & (k > 0))(lambda: pcopy(total, total, back, tot_s, tot_r, prv).start())
            pl.when((k > CEN + 1) & (k < last))(lambda: pcopy(total, total, back, tot_s, tot_r, nxt).start())

    def gated(buf, j):
        g = jnp.dot(recvd[...], buf[j, 0], preferred_element_type=jnp.float32)
        u = jnp.dot(recvd[...], buf[j, 1], preferred_element_type=jnp.float32)
        return g / (1.0 + jnp.exp(-g)) * u

    def own_block(j):
        own_hid[j] = gated(own, j).astype(jnp.bfloat16)

    def other_block(j):
        h = gated(oth, j)
        rows = lax.broadcasted_iota(jnp.int32, h.shape, 0)
        mix = jnp.where((rows & (ROWS - 1)) < ROWS // 2, own_hid[j].astype(jnp.float32), h)
        hid[j] = mix.astype(jnp.bfloat16)

    first = jnp.where(d == 0, 0, NJ - 1)
    second = NJ - 1 - first
    n2 = NB + 2 + jnp.maximum((last - 2 * k) * HOP + 6, 0)
    lag = jnp.where(k == last, LAG, 0)
    bound = jnp.maximum(count(k), n2 + 1)

    def mate_wait(s, _):
        cp(rel, oth, theirs(s), x_s, recv_d, mid).wait_recv()
        return 0

    def body(n, _):
        o = n + LEAD
        pl.when((k == 0) & (o < wopp))(lambda: opp_send(o).start())
        pl.when((k == last) & (n < count(0)))(lambda: first_send(n).wait_send())
        pl.when((k == last) & (o < count(0)))(lambda: first_send(o).start())
        s = n - lag

        @pl.when((s >= 0) & (s < count(k)))
        def _():
            c = mine(s)
            onward = (k < last) & (s < count(k + 1))
            direct = cp(oth, oth, c, fwd_d, recv_d, nxt)
            relayed = cp(rel, rel, c, fwd_r, recv_r, nxt)
            direct.wait_recv()
            pl.when(onward)(lambda: direct.start())
            relayed.wait_recv()
            pl.when(onward)(lambda: relayed.start())
            cp(rel, oth, c, x_s, recv_d, mid).start()

        pl.when(s >= 0)(lambda: deltas(s))
        pl.when((k < 8) & (n < PLANE - 1))(lambda: dispatch(n))

        @pl.when(s == NB - 3)
        def _():
            pltpu.make_async_copy(recvd.at[pl.ds(0, (PLANE - 1) * ROWS)], recvd.at[pl.ds(0, (PLANE - 1) * ROWS)], disp_r).wait()
            own_rows.wait()

        pl.when((s >= NB - 3) & (s < NB - 3 + NJ))(lambda: own_block(s - NB + 3))
        pl.when(s == NB)(lambda: other_block(first))

        @pl.when(s == n2)
        def _():
            lax.fori_loop(0, NB, mate_wait, 0)
            other_block(second)

        return 0

    lax.fori_loop(0, bound + lag, body, 0)
    lax.fori_loop(NB, M - count(k), mate_wait, 0)
    for j in range(1, NJ - 1):
        other_block(j)

    def give_back(n, _):
        q, dev = peer(n)
        pltpu.make_async_remote_copy(src_ref=hid.at[:, block(q)], dst_ref=ret.at[:, block(me)], send_sem=ret_s,
                                     recv_sem=ret_r, device_id=dev, device_id_type=MESH).start()
        return 0

    lax.fori_loop(0, PLANE - 1, give_back, 0)
    keep = pltpu.make_async_copy(hid.at[:, block(me)], ret.at[:, block(me)], loc_s.at[1])
    keep.start()

    def fin(s, _):
        c = mine(s)

        @pl.when((k < last) & (s < count(k + 1)))
        def _():
            cp(oth, oth, c, fwd_d, recv_d, nxt).wait_send()
            cp(rel, rel, c, fwd_r, recv_r, nxt).wait_send()

        pl.when(s < count(k))(lambda: cp(rel, oth, c, x_s, recv_d, mid).wait_send())
        pl.when((k == 0) & (s < wopp))(lambda: opp_send(s).wait_send())
        return 0

    lax.fori_loop(0, M // 2 + 2 * SHIFT + 1, fin, 0)
    pltpu.make_async_copy(outg.at[pl.ds(0, (PLANE - 1) * ROWS)], outg.at[pl.ds(0, (PLANE - 1) * ROWS)], disp_s).wait()
    for c in range(PIECES):
        pl.when((k != CEN) & (k != CEN + 1))(lambda: pcopy(acc, part, c, in_s, in_r, nxt).wait_send())
        pl.when((k == CEN) | (k == CEN + 1))(lambda: pcopy(acc, xin, c, xin_s, xin_r, nxt).wait_send())
        pl.when((k > 0) & (k < last))(lambda: pcopy(total, total, c, tot_s, tot_r, nxt).wait_send())

    others = pl.ds(0, (PLANE - 1) * ROWS)
    pltpu.make_async_copy(ret.at[:, others], ret.at[:, others], ret_r).wait()
    keep.wait()
    for t in range(2):
        for j in range(NJ):
            got = jnp.dot(pick[t], ret[j], preferred_element_type=jnp.float32)
            mixed[t, :, pl.ds(j * CB, CB)] = (weights[:, t:t + 1] * got).astype(jnp.bfloat16)
    pltpu.make_async_copy(hid.at[:, others], hid.at[:, others], ret_s).wait()


def shards(tokens, routes, route_weight, gate_weight, up_weight, local_params, base, momentum):
    frag, cols = base.shape
    wide = cols // PIECES
    bf, f32 = jnp.bfloat16, jnp.float32
    vmem = pl.BlockSpec(memory_space=pltpu.VMEM)
    hbm = pl.BlockSpec(memory_space=pl.ANY)
    sems = pltpu.SemaphoreType.DMA
    mixed, total = pl.pallas_call(
        kernel,
        out_shape=(jax.ShapeDtypeStruct((2, TOK, HW), bf), jax.ShapeDtypeStruct((PIECES, frag, wide), f32)),
        in_specs=[vmem, vmem, vmem, hbm, hbm, vmem, vmem],
        out_specs=(vmem, vmem),
        scratch_shapes=[
            pltpu.VMEM((NJ, 2, DW, CB), bf), pltpu.VMEM((NJ, 2, DW, CB), bf), pltpu.VMEM((NJ, 2, DW, CB), bf),
            pltpu.VMEM((PLANE * ROWS, DW), bf), pltpu.VMEM((PLANE * ROWS, DW), bf),
            pltpu.VMEM((NJ, PLANE * ROWS, CB), bf), pltpu.VMEM((NJ, PLANE * ROWS, CB), bf),
            pltpu.VMEM((NJ, PLANE * ROWS, CB), bf), pltpu.VMEM((2, TOK, PLANE * ROWS), bf),
            pltpu.VMEM((PIECES, frag, wide), f32), pltpu.VMEM((PIECES, frag, wide), f32), pltpu.VMEM((PIECES, frag, wide), f32),
            sems((NJ, 2)), sems((M,)), sems((M,)), sems((M,)), sems((M,)), sems((M,)), sems((M,)),
            sems, sems, sems, sems, sems((2,)),
            sems((PIECES,)), sems((PIECES,)), sems((PIECES,)), sems((PIECES,)), sems((PIECES,)), sems((PIECES,)),
        ],
        compiler_params=pltpu.CompilerParams(collective_id=0, has_side_effects=True, vmem_limit_bytes=56 << 20),
        cost_estimate=pl.CostEstimate(flops=8 * PLANE * ROWS * DW * HW, bytes_accessed=10 << 20, transcendentals=0),
    )(tokens[0], routes[0], route_weight[0], gate_weight[0], up_weight[0], local_params[0], base)
    mixed = mixed.transpose(1, 0, 2)[None]
    outer_grad = total.transpose(1, 0, 2).reshape(frag, cols) / LINE
    new_momentum = outer_beta * momentum + outer_grad
    new_base = base - outer_rate * (outer_grad + outer_beta * new_momentum)
    return (mixed, new_base, new_momentum)


def solution(mesh):
    in_specs = (
        P("replica", "expert", None),
        P("replica", "expert", None),
        P("replica", "expert", None),
        P("expert", None, None),
        P("expert", None, None),
        P("replica", "expert", None),
        P("expert", None),
        P("expert", None),
    )
    out_specs = (P("replica", "expert", None, None), P("expert", None), P("expert", None))
    return jax.shard_map(shards, mesh=mesh, in_specs=in_specs, out_specs=out_specs, check_vma=False)
```

```python
import jax
import jax.numpy as jnp
from jax import lax
from jax.experimental import pallas as pl
from jax.experimental.pallas import tpu as pltpu
from jax.sharding import PartitionSpec as P

MESH = pl.DeviceIdType.MESH
outer_rate = 0.7
outer_beta = 0.9

LINE = 16
PLANE = 32
ROWS = 16
TOK, DW, HW = 128, 2560, 768
CB = 256
NJ = HW // CB
CHUNK = 128
NR = DW // CHUNK
NB = 2 * NR
M = NJ * NB
SHIFT = 10
LEAD = 6
LAG = 50
PIECES = 4
CEN = 8
HOP = 3
DRAIN = 8


def received(a):
    return M // 2 + ((LINE - 1 - 2 * a) * SHIFT) // 8


def kernel(tok, routes, weights, gate_hbm, up_hbm, local, base, mixed, total,
           own, oth, rel, outg, recvd, rows_own, rows_oth, own_hid, hid, ret, pick, wide, part, acc, xin,
           load_sem, recv_d, recv_r, fwd_d, fwd_r, x_s, own_r,
           disp_s, disp_r, ret_s, ret_r, loc_s, in_r, in_s, xin_r, xin_s, tot_r, tot_s):
    i = lax.axis_index("replica")
    e = lax.axis_index("expert")
    d = lax.rem(e, 2)
    half = e // PLANE
    me = lax.rem(e, PLANE)
    flip = lax.rem(e + PLANE, 2 * PLANE)
    mate = e + 1 - 2 * d
    mflip = lax.rem(mate + PLANE, 2 * PLANE)
    last = LINE - 1
    k = jnp.where(d == 0, i, last - i)
    end = jnp.where(d == 0, last, 0)
    way = 1 - 2 * d
    ni = lax.rem(i + way + LINE, LINE)
    pi = lax.rem(i - way + LINE, LINE)
    nxt = (ni, jnp.where(i == end, flip, e))
    prv = (pi, jnp.where(i == last - end, flip, e))
    opp = (pi, mflip)
    mid = (i, mate)

    def count(a):
        return jnp.where(d == 0, received(a), M - received(last - a))

    wopp = jnp.where(d == 0, M - received(last), received(0))

    def peer(n):
        q = lax.rem(me + 1 + n, PLANE)
        return q, (i, half * PLANE + q)

    barrier = pltpu.get_barrier_semaphore()
    for dev in (nxt, prv):
        pl.semaphore_signal(barrier, inc=1, device_id=dev, device_id_type=MESH)

    @pl.when(k == 0)
    def _():
        pl.semaphore_signal(barrier, inc=1, device_id=opp, device_id_type=MESH)

    loads = []
    for j in (0, NJ - 1, *range(1, NJ - 1)):
        for g, ref in enumerate((gate_hbm, up_hbm)):
            loads.append(pltpu.make_async_copy(ref.at[:, pl.ds(j * CB, CB)], own.at[j, g], load_sem.at[j, g]))
    for copy in loads:
        copy.start()

    def greet(n, _):
        pl.semaphore_signal(barrier, inc=1, device_id=peer(n)[1], device_id_type=MESH)
        return 0

    lax.fori_loop(0, PLANE - 1, greet, 0)
    pl.semaphore_wait(barrier, PLANE + 1 + jnp.where(k == 0, 1, 0))
    for copy in loads[:4]:
        copy.wait()

    def at(buf, c):
        rows = pl.ds(pl.multiple_of(lax.rem(c, NB) // 2 * CHUNK, CHUNK), CHUNK)
        return buf.at[c // NB, lax.rem(c, 2), rows, :]

    def cp(src, dst, c, ss, rs, dev):
        return pltpu.make_async_remote_copy(src_ref=at(src, c), dst_ref=at(dst, c), send_sem=ss.at[c],
                                            recv_sem=rs.at[c], device_id=dev, device_id_type=MESH)

    def mine(s):
        return jnp.where(d == 0, s, M - 1 - s)

    def theirs(s):
        return jnp.where(d == 0, M - 1 - s, s)

    def opp_send(s):
        return cp(own, rel, theirs(s), own_r, recv_r, opp)

    def first_send(s):
        return cp(own, oth, mine(s), fwd_d, recv_d, nxt)

    def lead_body(s, _):
        pl.when(k == 0)(lambda: opp_send(s).start())
        pl.when(k == last)(lambda: first_send(s).start())
        return 0

    lax.fori_loop(0, LEAD, lead_body, 0)

    names = lax.broadcasted_iota(jnp.int32, (2 * PLANE, TOK), 0)
    r = [routes[0:1, :], routes[1:2, :]]
    named = ((r[0] == names) | (r[1] == names)).astype(jnp.float32)
    before = (lax.broadcasted_iota(jnp.int32, (TOK, TOK), 0) < lax.broadcasted_iota(jnp.int32, (TOK, TOK), 1))
    before = before.astype(jnp.float32)
    ranks = jnp.dot(named.astype(jnp.bfloat16), before.astype(jnp.bfloat16), preferred_element_type=jnp.float32)
    slots = lax.broadcasted_iota(jnp.int32, (PLANE * ROWS, TOK), 0)
    place = jnp.zeros((PLANE * ROWS, TOK), jnp.float32)
    for t in range(2):
        rank = jnp.sum(jnp.where(r[t] == names, ranks, 0.0), axis=0, keepdims=True).astype(jnp.int32)
        row = (r[t] & (PLANE - 1)) * ROWS + jnp.where(r[t] // PLANE == half, 0, ROWS // 2) + rank
        one = (row == slots).astype(jnp.float32)
        pick[t] = one.T.astype(jnp.bfloat16)
        wide[t] = jnp.broadcast_to(weights[t:t + 1, :], (TOK, TOK)).T
        place += one
    place_t = place.astype(jnp.bfloat16)
    for c in range(DW // 512):
        cols = pl.ds(c * 512, 512)
        outg[:, cols] = jnp.dot(place_t, tok[:, cols], preferred_element_type=jnp.float32).astype(jnp.bfloat16)

    def block(q):
        return pl.ds(pl.multiple_of(q * ROWS, ROWS), ROWS)

    def dispatch(n):
        q, dev = peer(n)
        pltpu.make_async_remote_copy(src_ref=outg.at[block(q)], dst_ref=recvd.at[block(me)], send_sem=disp_s,
                                     recv_sem=disp_r, device_id=dev, device_id_type=MESH).start()

    own_rows = pltpu.make_async_copy(outg.at[block(me)], recvd.at[block(me)], loc_s.at[0])
    own_rows.start()

    @pl.when(k >= 8)
    def _():
        def body(n, _):
            dispatch(n)
            return 0
        lax.fori_loop(0, PLANE - 1, body, 0)

    def pcopy(src, dst, c, ss, rs, dev):
        return pltpu.make_async_remote_copy(src_ref=src.at[c], dst_ref=dst.at[c], send_sem=ss.at[c],
                                            recv_sem=rs.at[c], device_id=dev, device_id_type=MESH)

    delta = (base[...] - local[...].astype(jnp.float32)).astype(jnp.bfloat16).astype(jnp.float32)
    acc[...] = delta.reshape(acc.shape)

    @pl.when(k > CEN)
    def _():
        for c in range(PIECES):
            @pl.when(k < last)
            def _():
                pcopy(acc, part, c, in_s, in_r, prv).wait_recv()
                acc[c] = acc[c] + part[c]

            pl.when(k > CEN + 1)(lambda: pcopy(acc, part, c, in_s, in_r, prv).start())
            pl.when(k == CEN + 1)(lambda: pcopy(acc, xin, c, xin_s, xin_r, prv).start())

    def deltas(s):
        low = k <= CEN

        @pl.when(low & (s < PIECES))
        def _():
            @pl.when(k > 0)
            def _():
                pcopy(acc, part, s, in_s, in_r, nxt).wait_recv()
                acc[s] = acc[s] + part[s]

            pl.when(k < CEN)(lambda: pcopy(acc, part, s, in_s, in_r, nxt).start())
            pl.when(k == CEN)(lambda: pcopy(acc, xin, s, xin_s, xin_r, nxt).start())

        meet = s - jnp.where(low, 6, 1)

        @pl.when(((k == CEN) | (k == CEN + 1)) & (meet >= 0) & (meet < PIECES))
        def _():
            pcopy(acc, xin, meet, xin_s, xin_r, nxt).wait_recv()
            total[meet] = acc[meet] + xin[meet]
            pl.when(low)(lambda: pcopy(total, total, meet, tot_s, tot_r, prv).start())
            pl.when(k > CEN)(lambda: pcopy(total, total, meet, tot_s, tot_r, nxt).start())

        back = s - jnp.where(low, 2 * HOP * (CEN - k) + 6, 2)

        @pl.when(((k < CEN) | (k > CEN + 1)) & (back >= 0) & (back < PIECES))
        def _():
            pcopy(total, total, back, tot_s, tot_r, prv).wait_recv()
            pl.when((k < CEN) & (k > 0))(lambda: pcopy(total, total, back, tot_s, tot_r, prv).start())
            pl.when((k > CEN + 1) & (k < last))(lambda: pcopy(total, total, back, tot_s, tot_r, nxt).start())

    def split():
        for c in range(DW // 512):
            cols = pl.ds(c * 512, 512)
            both = recvd[:, cols].astype(jnp.float32).reshape(PLANE, ROWS, 512)
            rows_own[:, cols] = both[:, :ROWS // 2].reshape(PLANE * ROWS // 2, 512).astype(jnp.bfloat16)
            rows_oth[:, cols] = both[:, ROWS // 2:].reshape(PLANE * ROWS // 2, 512).astype(jnp.bfloat16)

    def gated(rows, buf, j):
        g = jnp.dot(rows[...], buf[j, 0], preferred_element_type=jnp.float32)
        u = jnp.dot(rows[...], buf[j, 1], preferred_element_type=jnp.float32)
        return g / (1.0 + jnp.exp(-g)) * u

    def own_block(j):
        own_hid[j] = gated(rows_own, own, j)

    def other_block(j):
        h = gated(rows_oth, oth, j).reshape(PLANE, ROWS // 2, CB)
        both = jnp.concatenate([own_hid[j].reshape(PLANE, ROWS // 2, CB), h], axis=1)
        hid[j] = both.reshape(PLANE * ROWS, CB).astype(jnp.bfloat16)

    def give_back(n, j):
        q, dev = peer(n)
        pltpu.make_async_remote_copy(src_ref=hid.at[j, block(q)], dst_ref=ret.at[j, block(me)], send_sem=ret_s.at[j],
                                     recv_sem=ret_r.at[j], device_id=dev, device_id_type=MESH).start()

    def keep(j):
        return pltpu.make_async_copy(hid.at[j, block(me)], ret.at[j, block(me)], loc_s.at[1 + j])

    def give_all(j, begin):
        def body(n, _):
            give_back(n, j)
            return 0
        lax.fori_loop(begin, PLANE - 1, body, 0)
        keep(j).start()

    first = jnp.where(d == 0, 0, NJ - 1)
    second = NJ - 1 - first
    n2 = NB + 2 + jnp.maximum((last - 2 * k) * HOP + 6, 0)
    lag = jnp.where(k == last, LAG, 0)
    bound = jnp.maximum(count(k), n2 + 1)
    loads[4].wait()
    loads[5].wait()

    def mate_wait(s, _):
        cp(rel, oth, theirs(s), x_s, recv_d, mid).wait_recv()
        return 0

    def drain(s):
        c = mine(s)
        cp(rel, oth, c, x_s, recv_d, mid).wait_send()

        @pl.when((k < last) & (s < count(k + 1)))
        def _():
            cp(oth, oth, c, fwd_d, recv_d, nxt).wait_send()
            cp(rel, rel, c, fwd_r, recv_r, nxt).wait_send()

    def body(n, _):
        o = n + LEAD
        pl.when((k == 0) & (o < wopp))(lambda: opp_send(o).start())
        pl.when((k == last) & (n < count(0)))(lambda: first_send(n).wait_send())
        pl.when((k == last) & (o < count(0)))(lambda: first_send(o).start())
        s = n - lag

        @pl.when((s >= 0) & (s < count(k)))
        def _():
            c = mine(s)
            onward = (k < last) & (s < count(k + 1))
            direct = cp(oth, oth, c, fwd_d, recv_d, nxt)
            relayed = cp(rel, rel, c, fwd_r, recv_r, nxt)
            direct.wait_recv()
            pl.when(onward)(lambda: direct.start())
            relayed.wait_recv()
            pl.when(onward)(lambda: relayed.start())
            cp(rel, oth, c, x_s, recv_d, mid).start()
            pl.when(s >= DRAIN)(lambda: drain(s - DRAIN))

        pl.when((k == 0) & (n >= DRAIN) & (n < wopp))(lambda: opp_send(n - DRAIN).wait_send())
        pl.when(s >= 0)(lambda: deltas(s))
        pl.when((k < 8) & (n < PLANE - 1))(lambda: dispatch(n))

        @pl.when(s == NB - 4)
        def _():
            pltpu.make_async_copy(recvd.at[pl.ds(0, (PLANE - 1) * ROWS)], recvd.at[pl.ds(0, (PLANE - 1) * ROWS)], disp_r).wait()
            own_rows.wait()
            split()

        pl.when((s >= NB - 3) & (s < NB - 3 + NJ))(lambda: own_block(s - NB + 3))
        pl.when(s == NB)(lambda: other_block(first))
        pl.when((s > NB) & (s < NB + PLANE))(lambda: give_back(s - NB - 1, first))

        @pl.when(s == n2)
        def _():
            lax.fori_loop(0, NB, mate_wait, 0)
            other_block(second)
            give_all(second, 0)

        return 0

    lax.fori_loop(0, bound + lag, body, 0)
    give_all(first, jnp.minimum(bound - NB - 1, PLANE - 1))
    lax.fori_loop(NB, M - count(k), mate_wait, 0)
    for j in range(1, NJ - 1):
        other_block(j)
        give_all(j, 0)

    for n in range(DRAIN):
        drain(count(k) - DRAIN + n)
        pl.when(k == 0)(lambda: opp_send(wopp - DRAIN + n).wait_send())
    pltpu.make_async_copy(outg.at[pl.ds(0, (PLANE - 1) * ROWS)], outg.at[pl.ds(0, (PLANE - 1) * ROWS)], disp_s).wait()
    for c in range(PIECES):
        pl.when((k != CEN) & (k != CEN + 1))(lambda: pcopy(acc, part, c, in_s, in_r, nxt).wait_send())
        pl.when((k == CEN) | (k == CEN + 1))(lambda: pcopy(acc, xin, c, xin_s, xin_r, nxt).wait_send())
        pl.when((k > 0) & (k < last))(lambda: pcopy(total, total, c, tot_s, tot_r, nxt).wait_send())

    others = pl.ds(0, (PLANE - 1) * ROWS)

    def combine(j):
        pltpu.make_async_copy(ret.at[j, others], ret.at[j, others], ret_r.at[j]).wait()
        keep(j).wait()
        for t in range(2):
            got = jnp.dot(pick[t], ret[j], preferred_element_type=jnp.float32)
            mixed[t, :, pl.ds(pl.multiple_of(j * CB, CB), CB)] = (wide[t][:, 0:1] * got).astype(jnp.bfloat16)

    combine(first)
    combine(second)
    for j in range(1, NJ - 1):
        combine(j)
    for j in range(NJ):
        pltpu.make_async_copy(hid.at[j, others], hid.at[j, others], ret_s.at[j]).wait()


def shards(tokens, routes, route_weight, gate_weight, up_weight, local_params, base, momentum):
    frag, cols = base.shape
    bf, f32 = jnp.bfloat16, jnp.float32
    vmem = pl.BlockSpec(memory_space=pltpu.VMEM)
    hbm = pl.BlockSpec(memory_space=pl.ANY)
    sems = pltpu.SemaphoreType.DMA
    mixed, total = pl.pallas_call(
        kernel,
        out_shape=(jax.ShapeDtypeStruct((2, TOK, HW), bf), jax.ShapeDtypeStruct((PIECES, frag // PIECES, cols), f32)),
        in_specs=[vmem, vmem, vmem, hbm, hbm, vmem, vmem],
        out_specs=(vmem, vmem),
        scratch_shapes=[
            pltpu.VMEM((NJ, 2, DW, CB), bf), pltpu.VMEM((NJ, 2, DW, CB), bf), pltpu.VMEM((NJ, 2, DW, CB), bf),
            pltpu.VMEM((PLANE * ROWS, DW), bf), pltpu.VMEM((PLANE * ROWS, DW), bf),
            pltpu.VMEM((PLANE * ROWS // 2, DW), bf), pltpu.VMEM((PLANE * ROWS // 2, DW), bf),
            pltpu.VMEM((NJ, PLANE * ROWS // 2, CB), f32), pltpu.VMEM((NJ, PLANE * ROWS, CB), bf),
            pltpu.VMEM((NJ, PLANE * ROWS, CB), bf), pltpu.VMEM((2, TOK, PLANE * ROWS), bf), pltpu.VMEM((2, TOK, TOK), f32),
            pltpu.VMEM((PIECES, frag // PIECES, cols), f32), pltpu.VMEM((PIECES, frag // PIECES, cols), f32), pltpu.VMEM((PIECES, frag // PIECES, cols), f32),
            sems((NJ, 2)), sems((M,)), sems((M,)), sems((M,)), sems((M,)), sems((M,)), sems((M,)),
            sems, sems, sems((NJ,)), sems((NJ,)), sems((1 + NJ,)),
            sems((PIECES,)), sems((PIECES,)), sems((PIECES,)), sems((PIECES,)), sems((PIECES,)), sems((PIECES,)),
        ],
        compiler_params=pltpu.CompilerParams(collective_id=0, has_side_effects=True, vmem_limit_bytes=56 << 20),
        cost_estimate=pl.CostEstimate(flops=8 * PLANE * ROWS * DW * HW, bytes_accessed=10 << 20, transcendentals=0),
    )(tokens[0], routes[0].T, route_weight[0].T, gate_weight[0], up_weight[0], local_params[0], base)
    mixed = mixed.transpose(1, 0, 2)[None]
    outer_grad = total.reshape(frag, cols) / LINE
    new_momentum = outer_beta * momentum + outer_grad
    new_base = base - outer_rate * (outer_grad + outer_beta * new_momentum)
    return (mixed, new_base, new_momentum)


def solution(mesh):
    in_specs = (
        P("replica", "expert", None),
        P("replica", "expert", None),
        P("replica", "expert", None),
        P("expert", None, None),
        P("expert", None, None),
        P("replica", "expert", None),
        P("expert", None),
        P("expert", None),
    )
    out_specs = (P("replica", "expert", None, None), P("expert", None), P("expert", None))
    return jax.shard_map(shards, mesh=mesh, in_specs=in_specs, out_specs=out_specs, check_vma=False)
```
